512 devices in a mesh: thread: 64 (over z_lo, x, core), head: 8 (over z_hi, y).
Axes of the slice: x: 4, y: 4, z: 16 (z_hi: 2, z_lo: 8; z = z_hi * 8 + z_lo), core: 2. Of those that a mesh axis runs over, the one named last changes fastest.
Arguments:
- request_id: int32 [64], P('thread'), may hold values from 0 to 31, never falling along the last dimension, each value on 1 to 3 neighbouring positions
- cache_len: int32 [64], P('thread'), may hold values from 1 to 2048, 43690 in all
- query: bfloat16 [64, 64, 64, 128], P('thread', None, 'head'), may hold values from -6 to 6
- new_key: bfloat16 [64, 64, 8, 128], P('thread', None, 'head'), may hold values from -6 to 6
- new_value: bfloat16 [64, 64, 8, 128], P('thread', None, 'head'), may hold values from -8 to 8
- key_cache: bfloat16 [64, 2048, 8, 128], P('thread', None, 'head'), may hold values from -6 to 6
- value_cache: bfloat16 [64, 2048, 8, 128], P('thread', None, 'head'), may hold values from -5 to 5
- out_weight: bfloat16 [8192, 8192], P('head', 'thread'), may hold values from -0.0625 to 0.0625
Outputs:
- projected: bfloat16 [64, 64, 8192], P(None, 'head', 'thread')
The draws below stay inside these ranges and needn't reach their ends.
Inputs may be any that keep to these rules, and one draw needn't show every extreme that they name: `request_id`: never falling; each request holds 1 to 3 consecutive threads, and some request exactly 3. `cache_len`: some thread has exactly 2048 filled slots.
All inputs are finite; a program needn't handle non-finite values. No bound on the sum of `cache_len` on one device may be relied on, other than what follows from the above.
Results may differ from the reference program's by a relative error of at most 0.019.
Values may be sent and summed in bfloat16 or wider, within the bound.
No kernel may reach another device: no remote copies, remote signals or barrier semaphores. Data moves between devices by JAX's collectives and lax.ppermute only.
A program may use at most 64 MiB of HBM per device.

```python
import math
import jax
import jax.numpy as jnp
import numpy as np
from jax import lax

D = 8192
QH = 64
KVH = 8
HD = 128
STEP_TOK = 16
NEW = 64
CAP = 2048
G_MAX = 3
THREADS = 64


def draw_query(key, part):
    key = jax.random.fold_in(key, 1)
    full_shape = (THREADS, NEW, QH, HD)
    base = jnp.clip(jax.random.normal(key, full_shape, jnp.float32), -6.0, 6.0)
    return base.astype(jnp.bfloat16)


def draw_new_key(key, part):
    key = jax.random.fold_in(key, 2)
    full_shape = (THREADS, NEW, KVH, HD)
    base = jnp.clip(jax.random.normal(key, full_shape, jnp.float32), -6.0, 6.0)
    return base.astype(jnp.bfloat16)


def draw_value_cache(key, part):
    key = jax.random.fold_in(key, 3)
    mean_key, noise_key = jax.random.split(key)
    full_shape = (THREADS, CAP, KVH, HD)
    means = jax.random.normal(mean_key, (THREADS, 1, KVH, HD), jnp.float32)
    noise = 0.5 * jax.random.normal(noise_key, full_shape, jnp.float32)
    return jnp.clip(means + noise, -5.0, 5.0).astype(jnp.bfloat16)


def block_levels(stream_key, dims, shards, least, largest):
    def one(dim, shards_of):
        draws = jax.random.uniform(jax.random.fold_in(jax.random.fold_in(stream_key, 6), dim), (shards_of,), jnp.float32, least / len(shards), largest / len(shards))
        return jnp.repeat(jnp.exp(draws), dims[dim] // shards_of).reshape((-1,) + (1,) * (len(dims) - dim - 1))

    loudness = one(*shards[0])
    for cut in shards[1:]:
        loudness = loudness * one(*cut)
    return loudness


def length_profile(count, total, reach, lean):
    portions = [(1 << 20) // math.isqrt(standing ** lean) + 1 for standing in range(2, count + 1)]
    surplus, counts = total - reach - (count - 1), [1] * (count - 1)
    while surplus > 0:
        free = [i for i in range(count - 1) if counts[i] < reach]
        whole, budget = sum([portions[i] for i in free]), surplus
        for i in free:
            more = min(reach - counts[i], max(1, budget * portions[i] // whole), surplus)
            counts[i] = counts[i] + more
            surplus = surplus - more
    return np.array([reach] + counts)


def uneven(key, count, total, most, lean):
    if count == 2:
        one = jax.random.randint(key, (), max(1, total - most), min(most, total - 1) + 1)
        return jnp.stack([one, total - one])
    lengths = jnp.asarray(length_profile(count, total, most, lean), jnp.int32)
    pairs = (count - 1) // 2
    giver, taker = lengths[1:1 + 2 * pairs:2], lengths[2:2 + 2 * pairs:2]
    room = jnp.minimum(giver - 1, most - taker)
    shifted = jax.random.randint(jax.random.fold_in(key, 1), (pairs,), 0, 1 << 20) % (room + 1)
    lengths = lengths.at[1:1 + 2 * pairs:2].set(giver - shifted).at[2:2 + 2 * pairs:2].set(taker + shifted)
    return lengths[jax.random.permutation(jax.random.fold_in(key, 2), count)]


def centred(rng, extent, width, reach, cuts=(), kind=jnp.bfloat16):
    factor_of = block_levels(rng, extent, cuts, -0.22, 0.18) if cuts else 1.0
    values = jax.random.normal(rng, extent, jnp.float32) * width * factor_of
    return jnp.minimum(jnp.maximum(values, -reach), reach).astype(kind)


def setup_inputs(seed: int = 0) -> dict:
    arg_keys = jax.random.split(jax.random.key(seed), 9)
    return {
        "request_id": jnp.searchsorted(jnp.cumsum(uneven(arg_keys[0], THREADS // 2, THREADS, G_MAX, 2)), jnp.arange(THREADS), side="right").astype(jnp.int32),
        "cache_len": uneven(arg_keys[1], THREADS, THREADS * CAP // 3, CAP, 2).astype(jnp.int32),
        "query": draw_query(jax.random.fold_in(arg_keys[8], 71), 0),
        "new_key": draw_new_key(jax.random.fold_in(arg_keys[8], 71), 0),
        "new_value": centred(arg_keys[4], (THREADS, NEW, KVH, HD), 2.0, 8.0, ((0, 64), (2, 8))),
        "key_cache": centred(arg_keys[5], (THREADS, CAP, KVH, HD), 1.0, 6.0, ((0, 64), (2, 8))),
        "value_cache": draw_value_cache(jax.random.fold_in(arg_keys[8], 71), 0),
        "out_weight": centred(arg_keys[7], (QH * HD, D), (QH * HD) ** -0.5, 0.0625, ((0, 8), (1, 64))),
    }


def reference(request_id, cache_len, query, new_key, new_value, key_cache, value_cache, out_weight):
    thread_count, new_count, query_heads, head_dim = query.shape
    capacity = key_cache.shape[1]
    kv_heads = key_cache.shape[2]
    group_size = query_heads // kv_heads
    row_count = new_count * group_size
    factor = head_dim ** -0.5
    row_token = jnp.arange(row_count, dtype=jnp.int32) // group_size
    key_token = jnp.arange(new_count, dtype=jnp.int32)
    positions = jnp.arange(capacity, dtype=jnp.int32)

    def one_thread(thread):
        queries = query[thread].astype(jnp.float32).reshape(new_count, kv_heads, group_size, head_dim)
        queries = queries.transpose(1, 0, 2, 3).reshape(kv_heads, row_count, head_dim)
        key_parts = []
        value_parts = []
        allow_parts = []
        for offset in range(-(G_MAX - 1), G_MAX):
            other = thread + offset
            inside = (other >= 0) & (other < thread_count)
            clipped = jnp.clip(other, 0, thread_count - 1).astype(jnp.int32)
            sibling = inside & (request_id[clipped] == request_id[thread])
            key_parts += [key_cache[clipped], new_key[clipped]]
            value_parts += [value_cache[clipped], new_value[clipped]]
            cache_ok = jnp.broadcast_to((positions < cache_len[clipped])[None, :] & sibling, (row_count, capacity))
            if offset == 0:
                new_ok = key_token[None, :] <= row_token[:, None]
            else:
                new_ok = (key_token[None, :] // STEP_TOK < row_token[:, None] // STEP_TOK) & sibling
            allow_parts += [cache_ok, new_ok]
        key_rows = jnp.concatenate(key_parts, axis=0).astype(jnp.float32)
        value_rows = jnp.concatenate(value_parts, axis=0).astype(jnp.float32)
        allowed = jnp.concatenate(allow_parts, axis=1)
        scores = jnp.einsum("hrd,khd->hrk", queries, key_rows) * factor
        scores = jnp.where(allowed[None], scores, -1e30)
        row_max = jnp.max(scores, axis=-1)
        weights = jnp.where(allowed[None], jnp.exp(scores - row_max[..., None]), 0.0)
        row_total = jnp.sum(weights, axis=-1)
        rounded = lax.optimization_barrier(weights.astype(jnp.bfloat16)).astype(jnp.float32)
        summed = jnp.einsum("hrk,khd->hrd", rounded, value_rows)
        attended = (summed / row_total[..., None]).reshape(kv_heads, new_count, group_size, head_dim)
        attended = attended.transpose(1, 0, 2, 3).reshape(new_count, query_heads * head_dim)
        return attended.astype(jnp.bfloat16)

    attended = lax.map(one_thread, jnp.arange(thread_count, dtype=jnp.int32))
    projected = jnp.dot(attended.reshape(thread_count * new_count, query_heads * head_dim), out_weight, preferred_element_type=jnp.float32)
    return projected.reshape(thread_count, new_count, out_weight.shape[1]).astype(jnp.bfloat16)
```

```python
import functools

import jax
import jax.numpy as jnp
from jax import lax
from jax.experimental import pallas as pl
from jax.experimental.pallas import tpu as pltpu
from jax.sharding import PartitionSpec as P

STEP_TOK = 16
NEGATIVE = -1e30
LOG2_E = 1.4426950408889634
VMEM_LIMIT = 40 * 1024 * 1024

FINE = (("zh", 4), ("zl", 2), ("x", 4), ("c", 2), ("w", 2), ("y", 4))
THREAD = ("zh", "zl", "x", "c")
HEAD = ("w", "y")

BLOCK = 256
PAD = 16
LANES = 128


def diagonal(size):
    rows = lax.broadcasted_iota(jnp.int32, (size, size), 0)
    return rows == lax.broadcasted_iota(jnp.int32, (size, size), 1)


def attend_block(queries, first_row, keys, values, fresh_keys, fresh_values, length, is_own):
    factor = queries.shape[1] ** (-0.5)
    contract = (((1,), (1,)), ((), ()))
    cached = lax.dot_general(queries, keys, contract, preferred_element_type=jnp.float32)
    fresh = lax.dot_general(queries, fresh_keys, contract, preferred_element_type=jnp.float32)
    position = lax.broadcasted_iota(jnp.int32, cached.shape, 1)
    cached = jnp.where(position < length, cached, NEGATIVE)
    new_count = fresh.shape[1]
    token = (first_row + lax.broadcasted_iota(jnp.int32, fresh.shape, 0)) % new_count
    key_token = lax.broadcasted_iota(jnp.int32, fresh.shape, 1)
    if is_own:
        allowed = key_token <= token
    else:
        allowed = key_token // STEP_TOK < token // STEP_TOK
    fresh = jnp.where(allowed, fresh, NEGATIVE)
    row_max = jnp.maximum(
        jnp.max(cached, axis=1, keepdims=True), jnp.max(fresh, axis=1, keepdims=True)
    )
    cached = jnp.exp2((cached - row_max) * (factor * LOG2_E))
    fresh = jnp.exp2((fresh - row_max) * (factor * LOG2_E))
    total = jnp.sum(cached, axis=1, keepdims=True) + jnp.sum(fresh, axis=1, keepdims=True)
    summed = jnp.dot(cached.astype(jnp.bfloat16), values, preferred_element_type=jnp.float32)
    summed += jnp.dot(fresh.astype(jnp.bfloat16), fresh_values, preferred_element_type=jnp.float32)
    return summed / total, row_max * factor + jnp.log(total)


def own_kernel(length_ref, query_ref, key_ref, value_ref, new_key_ref, new_value_ref, out_ref, log_ref):
    for start in range(0, out_ref.shape[0], BLOCK):
        block = pl.ds(start, BLOCK)
        result, log_total = attend_block(
            query_ref[block], start, key_ref[...], value_ref[...], new_key_ref[...],
            new_value_ref[...], length_ref[0], True,
        )
        out_ref[block] = result
        log_ref[block] = jnp.broadcast_to(log_total, result.shape)


def same_request(own_ref, other_ref):
    return jnp.max(jnp.abs(own_ref[...].astype(jnp.float32) - other_ref[...].astype(jnp.float32))) == 0.0


def near_kernel(
    length_ref, own_tag_ref, key_ref, value_ref, new_key_ref, new_value_ref, *refs
):
    count = len(refs) // 2
    rows = refs[0].shape[0] - PAD
    for query_ref, out_ref in zip(refs[:count], refs[count:]):
        sibling = same_request(own_tag_ref, query_ref.at[pl.ds(rows, PAD)])

        @pl.when(sibling)
        def _():
            lines = []
            for start in range(0, rows, BLOCK):
                result, log_total = attend_block(
                    query_ref[pl.ds(start, BLOCK)], start, key_ref[...], value_ref[...],
                    new_key_ref[...], new_value_ref[...], length_ref[0], False,
                )
                out_ref[pl.ds(start, BLOCK)] = result.astype(out_ref.dtype)
                for piece in range(0, BLOCK, LANES):
                    column = jnp.broadcast_to(log_total[piece : piece + LANES], (LANES, LANES))
                    lines.append(
                        jnp.sum(jnp.where(diagonal(LANES), column, 0.0), axis=0, keepdims=True)
                    )
            exact = jnp.concatenate(lines, axis=0)
            high = exact.astype(jnp.bfloat16).astype(jnp.float32)
            middle = (exact - high).astype(jnp.bfloat16).astype(jnp.float32)
            low = exact - high - middle
            parts = jnp.concatenate([high, middle, low, jnp.zeros_like(low)], axis=0)
            out_ref[pl.ds(rows, PAD)] = parts.astype(out_ref.dtype)

        @pl.when(jnp.logical_not(sibling))
        def _():
            out_ref[...] = jnp.zeros_like(out_ref)


def merge_kernel(own_tag_ref, own_ref, own_log_ref, *refs):
    count = (len(refs) - 1) // 2
    tag_refs, part_refs, out_ref = refs[:count], refs[count:-1], refs[-1]
    rows = own_ref.shape[0]
    tokens = out_ref.shape[0]
    lines = rows // LANES
    siblings, logs = [], []
    for tag_ref, part_ref in zip(tag_refs, part_refs):
        siblings.append(same_request(own_tag_ref, tag_ref))
        pieces = part_ref[pl.ds(rows, PAD)].astype(jnp.float32)
        exact = pieces[:lines] + pieces[lines : 2 * lines] + pieces[2 * lines : 3 * lines]
        logs.append(jnp.where(siblings[-1], exact, NEGATIVE))
    for line in range(lines):
        block = pl.ds(line * LANES, LANES)
        columns = [own_log_ref[block]]
        terms = [own_ref[block]]
        for sibling, log_total, part_ref in zip(siblings, logs, part_refs):
            spread = jnp.broadcast_to(log_total[line : line + 1], (LANES, LANES))
            column = jnp.sum(jnp.where(diagonal(LANES), spread, 0.0), axis=1, keepdims=True)
            columns.append(jnp.broadcast_to(column, (LANES, LANES)))
            terms.append(jnp.where(sibling, part_ref[block].astype(jnp.float32), 0.0))
        largest = functools.reduce(jnp.maximum, columns)
        shares = [jnp.exp(column - largest) for column in columns]
        total = functools.reduce(jnp.add, shares)
        summed = functools.reduce(jnp.add, [share * term for share, term in zip(shares, terms)])
        merged = (summed / total).astype(out_ref.dtype)
        for piece in range(0, LANES, tokens):
            group = (line * LANES + piece) // tokens
            out_ref[:, pl.ds(group * LANES, LANES)] = merged[piece : piece + tokens]


def project_kernel(core_ref, near_ref, far_ref, weight_ref, out_ref):
    threads, tokens, feats = near_ref.shape
    y_size, w_size, z_size = out_ref.shape[:3]
    piece = tokens // (y_size * w_size)
    span = threads * piece
    for features, core in ((near_ref, core_ref[0]), (far_ref, 1 - core_ref[0])):
        place = pl.ds(pl.multiple_of(core * span, span), span)
        lines = features[...].reshape(threads * tokens, feats)
        for pair in range(0, z_size, 2):
            weights = jnp.concatenate([weight_ref[pair], weight_ref[pair + 1]], axis=1)
            terms = jnp.dot(lines, weights, preferred_element_type=jnp.float32)
            terms = terms.reshape(threads, w_size, y_size, piece, 2 * LANES)
            for y in range(y_size):
                for w in range(w_size):
                    part = terms[:, w, y].reshape(span, 2 * LANES).astype(out_ref.dtype)
                    out_ref[y, w, pair, place] = part[:, :LANES]
                    out_ref[y, w, pair + 1, place] = part[:, LANES:]


def on_chip(count):
    return [pl.BlockSpec(memory_space=pltpu.VMEM)] * count


SCALAR = pl.BlockSpec(memory_space=pltpu.SMEM)
PARAMS = pltpu.CompilerParams(vmem_limit_bytes=VMEM_LIMIT)


def neighbours():
    count = 1
    for name in THREAD:
        count *= lax.axis_size(name)
    up = [(i, i + 2) for i in range(count - 2)]
    down = [(i + 2, i) for i in range(count - 2)]
    across = [pair for i in range(1, count - 1, 2) for pair in ((i, i + 1), (i + 1, i))]
    beside = [pair for i in range(0, count, 2) for pair in ((i, i + 1), (i + 1, i))]
    return (up, down, across, beside), (1, 0, 2, 3)


def project(attended, out_weight, weights):
    tokens, feats = attended.shape
    y_size, w_size, z_size = lax.axis_size("y"), lax.axis_size("w"), lax.axis_size("zh")
    threads, cores = lax.axis_size("zl") * lax.axis_size("x"), lax.axis_size("c")
    piece = tokens // (y_size * w_size)
    spread = jnp.broadcast_to(attended[None], (threads, tokens, feats))
    near = lax.all_to_all(spread, ("zl", "x"), 0, 0)
    far = lax.ppermute(near, "c", [(0, 1), (1, 0)])
    core = lax.axis_index("c").astype(jnp.int32).reshape(1)
    columns = out_weight.shape[1]
    terms = pl.pallas_call(
        project_kernel,
        out_shape=jax.ShapeDtypeStruct(
            (y_size, w_size, z_size, cores * threads * piece, columns), jnp.bfloat16
        ),
        in_specs=[SCALAR] + on_chip(3),
        out_specs=on_chip(1)[0],
        compiler_params=PARAMS,
        name="project",
    )(core, near, far, weights)
    terms = lax.all_to_all(terms, "y", 0, 0)
    terms = jnp.sum(terms.astype(jnp.float32), axis=0).astype(jnp.bfloat16)
    terms = lax.all_to_all(
        terms.reshape((w_size * z_size,) + terms.shape[2:]), ("w", "zh"), 0, 0
    ).reshape(terms.shape)
    result = jnp.sum(terms.astype(jnp.float32), axis=0).astype(jnp.bfloat16)
    result = result.reshape(z_size, cores, threads, piece, columns).transpose(0, 2, 1, 3, 4)
    return result.reshape(z_size * threads * cores, piece, columns)


def body(request_id, cache_len, query, new_key, new_value, key_cache, value_cache, out_weight):
    new_count, group_size, head_dim = query.shape[1:]
    rows = new_count * group_size
    weights = lax.all_gather(out_weight, "zh", axis=0)
    by_head = query[0].transpose(1, 0, 2).reshape(rows, head_dim)
    tag = jnp.broadcast_to((request_id[0] + 1).astype(jnp.bfloat16), (PAD, head_dim))
    packed = jnp.concatenate([by_head, tag], axis=0)
    ways, back = neighbours()
    arrived = [lax.ppermute(packed, THREAD, way) for way in ways]
    caches = (key_cache[0, :, 0], value_cache[0, :, 0], new_key[0, :, 0], new_value[0, :, 0])
    own, own_log = pl.pallas_call(
        own_kernel,
        out_shape=[jax.ShapeDtypeStruct((rows, head_dim), jnp.float32)] * 2,
        in_specs=[SCALAR] + on_chip(5),
        out_specs=on_chip(2),
        compiler_params=PARAMS,
        name="own",
    )(cache_len, by_head, *caches)
    parts = pl.pallas_call(
        near_kernel,
        out_shape=[jax.ShapeDtypeStruct(packed.shape, jnp.bfloat16)] * len(ways),
        in_specs=[SCALAR] + on_chip(5 + len(ways)),
        out_specs=on_chip(len(ways)),
        compiler_params=PARAMS,
        name="near",
    )(cache_len, tag, *caches, *arrived)
    returned = [lax.ppermute(parts[back[way]], THREAD, ways[way]) for way in range(len(ways))]
    tags = [one[rows:] for one in arrived]
    attended = pl.pallas_call(
        merge_kernel,
        out_shape=jax.ShapeDtypeStruct((new_count, group_size * head_dim), jnp.bfloat16),
        in_specs=on_chip(3 + 2 * len(ways)),
        out_specs=on_chip(1)[0],
        compiler_params=PARAMS,
        name="merge",
    )(tag, own, own_log, *tags, *returned)
    return project(attended, out_weight, weights)


def solution(mesh):
    fine = jax.sharding.Mesh(
        mesh.devices.reshape([size for _, size in FINE]), [name for name, _ in FINE]
    )
    placed = (
        P(THREAD),
        P(THREAD),
        P(THREAD, None, HEAD, None),
        P(THREAD, None, HEAD, None),
        P(THREAD, None, HEAD, None),
        P(THREAD, None, HEAD, None),
        P(THREAD, None, HEAD, None),
        P(HEAD, THREAD),
    )
    return jax.shard_map(
        body, mesh=fine, in_specs=placed, out_specs=P(None, HEAD, THREAD), check_vma=False
    )
```

```python
import functools

import jax
import jax.numpy as jnp
from jax import lax
from jax.experimental import pallas as pl
from jax.experimental.pallas import tpu as pltpu
from jax.sharding import PartitionSpec as P

STEP_TOK = 16
NEGATIVE = -1e30
LOG2_E = 1.4426950408889634
VMEM_LIMIT = 40 * 1024 * 1024

FINE = (("zt", 2), ("zm", 2), ("zl", 2), ("x", 4), ("c", 2), ("w", 2), ("y", 4))
THREAD = ("zt", "zm", "zl", "x", "c")
HEAD = ("w", "y")

BLOCK = 256
PAD = 16
LANES = 128


def diagonal(size):
    rows = lax.broadcasted_iota(jnp.int32, (size, size), 0)
    return rows == lax.broadcasted_iota(jnp.int32, (size, size), 1)


def attend_block(queries, first_row, keys, values, fresh_keys, fresh_values, length, is_own):
    factor = queries.shape[1] ** (-0.5)
    contract = (((1,), (1,)), ((), ()))
    cached = lax.dot_general(queries, keys, contract, preferred_element_type=jnp.float32)
    fresh = lax.dot_general(queries, fresh_keys, contract, preferred_element_type=jnp.float32)
    position = lax.broadcasted_iota(jnp.int32, cached.shape, 1)
    cached = jnp.where(position < length, cached, NEGATIVE)
    new_count = fresh.shape[1]
    token = (first_row + lax.broadcasted_iota(jnp.int32, fresh.shape, 0)) % new_count
    key_token = lax.broadcasted_iota(jnp.int32, fresh.shape, 1)
    if is_own:
        allowed = key_token <= token
    else:
        allowed = key_token // STEP_TOK < token // STEP_TOK
    fresh = jnp.where(allowed, fresh, NEGATIVE)
    row_max = jnp.maximum(
        jnp.max(cached, axis=1, keepdims=True), jnp.max(fresh, axis=1, keepdims=True)
    )
    cached = jnp.exp2((cached - row_max) * (factor * LOG2_E))
    fresh = jnp.exp2((fresh - row_max) * (factor * LOG2_E))
    total = jnp.sum(cached, axis=1, keepdims=True) + jnp.sum(fresh, axis=1, keepdims=True)
    summed = jnp.dot(cached.astype(jnp.bfloat16), values, preferred_element_type=jnp.float32)
    summed += jnp.dot(fresh.astype(jnp.bfloat16), fresh_values, preferred_element_type=jnp.float32)
    return summed / total, row_max * factor + jnp.log(total)


def load(pairs, sems):
    copies = [pltpu.make_async_copy(src, dst, sems.at[i]) for i, (src, dst) in enumerate(pairs)]
    for copy in copies:
        copy.start()
    return copies


def own_kernel(
    length_ref, query_ref, key_hbm, value_hbm, new_key_hbm, new_value_hbm, out_ref, log_ref,
    key_ref, value_ref, new_key_ref, new_value_ref, sems,
):
    for copy in load(
        ((key_hbm, key_ref), (value_hbm, value_ref), (new_key_hbm, new_key_ref), (new_value_hbm, new_value_ref)), sems
    ):
        copy.wait()
    for start in range(0, out_ref.shape[0], BLOCK):
        block = pl.ds(start, BLOCK)
        result, log_total = attend_block(
            query_ref[block], start, key_ref[...], value_ref[...], new_key_ref[...],
            new_value_ref[...], length_ref[0], True,
        )
        out_ref[block] = result
        log_ref[block] = jnp.broadcast_to(log_total, result.shape)


def same_request(own_ref, other_ref):
    return jnp.max(jnp.abs(own_ref[...].astype(jnp.float32) - other_ref[...].astype(jnp.float32))) == 0.0


def near_kernel(length_ref, own_tag_ref, key_hbm, value_hbm, new_key_hbm, new_value_hbm, *refs):
    *refs, key_ref, value_ref, new_key_ref, new_value_ref, sems = refs
    for copy in load(
        ((key_hbm, key_ref), (value_hbm, value_ref), (new_key_hbm, new_key_ref), (new_value_hbm, new_value_ref)), sems
    ):
        copy.wait()
    count = len(refs) // 2
    rows = refs[0].shape[0] - PAD
    for query_ref, out_ref in zip(refs[:count], refs[count:]):
        sibling = same_request(own_tag_ref, query_ref.at[pl.ds(rows, PAD)])

        @pl.when(sibling)
        def _():
            lines = []
            for start in range(0, rows, BLOCK):
                result, log_total = attend_block(
                    query_ref[pl.ds(start, BLOCK)], start, key_ref[...], value_ref[...],
                    new_key_ref[...], new_value_ref[...], length_ref[0], False,
                )
                out_ref[pl.ds(start, BLOCK)] = result.astype(out_ref.dtype)
                for piece in range(0, BLOCK, LANES):
                    column = jnp.broadcast_to(log_total[piece : piece + LANES], (LANES, LANES))
                    lines.append(
                        jnp.sum(jnp.where(diagonal(LANES), column, 0.0), axis=0, keepdims=True)
                    )
            exact = jnp.concatenate(lines, axis=0)
            high = exact.astype(jnp.bfloat16).astype(jnp.float32)
            middle = (exact - high).astype(jnp.bfloat16).astype(jnp.float32)
            low = exact - high - middle
            parts = jnp.concatenate([high, middle, low, jnp.zeros_like(low)], axis=0)
            out_ref[pl.ds(rows, PAD)] = parts.astype(out_ref.dtype)

        @pl.when(jnp.logical_not(sibling))
        def _():
            out_ref[...] = jnp.zeros_like(out_ref)


def merge_kernel(ways, own_tag_ref, own_ref, own_log_ref, *refs):
    tag_refs, part_refs, weight_refs = refs[:ways], refs[ways : 2 * ways], refs[2 * ways : -3]
    out_ref, stack_ref, sems = refs[-3:]
    copies = load(
        [(ref, stack_ref.at[copy, i]) for copy in range(stack_ref.shape[0]) for i, ref in enumerate(weight_refs)],
        sems,
    )
    rows = own_ref.shape[0]
    tokens = out_ref.shape[0]
    lines = rows // LANES
    siblings, logs = [], []
    for tag_ref, part_ref in zip(tag_refs, part_refs):
        siblings.append(same_request(own_tag_ref, tag_ref))
        pieces = part_ref[pl.ds(rows, PAD)].astype(jnp.float32)
        exact = pieces[:lines] + pieces[lines : 2 * lines] + pieces[2 * lines : 3 * lines]
        logs.append(jnp.where(siblings[-1], exact, NEGATIVE))
    for line in range(lines):
        block = pl.ds(line * LANES, LANES)
        columns = [own_log_ref[block]]
        terms = [own_ref[block]]
        for sibling, log_total, part_ref in zip(siblings, logs, part_refs):
            spread = jnp.broadcast_to(log_total[line : line + 1], (LANES, LANES))
            column = jnp.sum(jnp.where(diagonal(LANES), spread, 0.0), axis=1, keepdims=True)
            columns.append(jnp.broadcast_to(column, (LANES, LANES)))
            terms.append(jnp.where(sibling, part_ref[block].astype(jnp.float32), 0.0))
        largest = functools.reduce(jnp.maximum, columns)
        shares = [jnp.exp(column - largest) for column in columns]
        total = functools.reduce(jnp.add, shares)
        summed = functools.reduce(jnp.add, [share * term for share, term in zip(shares, terms)])
        merged = (summed / total).astype(out_ref.dtype)
        for piece in range(0, LANES, tokens):
            group = (line * LANES + piece) // tokens
            out_ref[:, pl.ds(group * LANES, LANES)] = merged[piece : piece + tokens]
    for copy in copies:
        copy.wait()


def project_kernel(place_ref, weight_ref, *refs):
    piece_refs, (out_ref, lines_ref) = refs[:-2], refs[-2:]
    pieces, (tokens, feats) = len(piece_refs), piece_refs[0].shape
    y_size, w_size = out_ref.shape[2:4]
    piece = tokens // (y_size * w_size)
    span = pieces * piece
    for index, piece_ref in enumerate(piece_refs):
        first = pl.multiple_of((place_ref[0] ^ index) * tokens, tokens)
        lines_ref[pl.ds(first, tokens)] = piece_ref[...]
    for x in range(weight_ref.shape[0]):
        weights = jnp.concatenate([weight_ref[x, 0], weight_ref[x, 1]], axis=1)
        terms = jnp.dot(lines_ref[...], weights, preferred_element_type=jnp.float32)
        terms = terms.reshape(pieces, w_size, y_size, piece, 2 * LANES)
        for y in range(y_size):
            for w in range(w_size):
                far = place_ref[2] ^ w
                part = terms[:, w, y].reshape(span, 2 * LANES).astype(out_ref.dtype)
                for side in range(2):
                    out_ref[place_ref[1] ^ side ^ far, x, y, far] = part[:, side * LANES : (side + 1) * LANES]


def on_chip(count):
    return [pl.BlockSpec(memory_space=pltpu.VMEM)] * count


IN_HBM = pl.BlockSpec(memory_space=pltpu.HBM)
SCALAR = pl.BlockSpec(memory_space=pltpu.SMEM)
PARAMS = pltpu.CompilerParams(vmem_limit_bytes=VMEM_LIMIT)


def neighbours():
    count = 1
    for name in THREAD:
        count *= lax.axis_size(name)
    up = [(i, i + 2) for i in range(count - 2)]
    down = [(i + 2, i) for i in range(count - 2)]
    across = [pair for i in range(1, count - 1, 2) for pair in ((i, i + 1), (i + 1, i))]
    beside = [pair for i in range(0, count, 2) for pair in ((i, i + 1), (i + 1, i))]
    return (up, down, across, beside), (1, 0, 2, 3)


def swap(value, axis, bit):
    names = (axis,) if isinstance(axis, str) else axis
    count = 1
    for name in names:
        count *= lax.axis_size(name)
    return lax.ppermute(value, axis, [(i, i ^ bit) for i in range(count)])


def project(attended, stack):
    tokens = attended.shape[0]
    size = {name: count for name, count in FINE}
    at = {name: lax.axis_index(name) for name in size}
    weights = lax.all_to_all(stack, "x", 0, 0)
    over_t, over_m = swap(attended, "zt", 1), swap(attended, "zm", 1)
    near = (attended, over_m, over_t, swap(over_t, "zm", 1))
    pieces = [piece for one in near for piece in (one, swap(one, "c", 1))]
    place = jnp.stack([at["zt"] * 4 + at["zm"] * 2 + at["c"], at["zl"], at["w"]]).astype(jnp.int32)
    piece, columns = tokens // (size["y"] * size["w"]), weights.shape[-1]
    block = (size["zl"], size["x"], size["y"], size["w"], len(pieces) * piece, columns)
    terms = pl.pallas_call(
        project_kernel,
        out_shape=jax.ShapeDtypeStruct(block, jnp.bfloat16),
        in_specs=[SCALAR] + on_chip(1 + len(pieces)),
        out_specs=on_chip(1)[0],
        scratch_shapes=[pltpu.VMEM((len(pieces) * tokens, attended.shape[1]), jnp.bfloat16)],
        compiler_params=PARAMS,
        name="project",
    )(place, weights, *pieces)
    terms = lax.all_to_all(terms.reshape((-1,) + block[3:]), ("zl", "x", "y"), 0, 0).reshape(block)
    terms = jnp.sum(terms.astype(jnp.float32), axis=2)
    arrived = swap(terms[:, :, 1].astype(jnp.bfloat16), ("zl", "w"), 3)
    result = (terms[:, :, 0] + arrived.astype(jnp.float32)).astype(jnp.bfloat16)
    result = result.reshape(
        size["zl"], size["x"], size["zt"], size["zm"], size["c"], piece, columns
    )
    return result.transpose(2, 3, 0, 1, 4, 5, 6).reshape(-1, piece, columns)


def body(request_id, cache_len, query, new_key, new_value, key_cache, value_cache, out_weight):
    new_count, group_size, head_dim = query.shape[1:]
    rows = new_count * group_size
    by_head = query[0].transpose(1, 0, 2).reshape(rows, head_dim)
    tag = jnp.broadcast_to((request_id[0] + 1).astype(jnp.bfloat16), (PAD, head_dim))
    packed = jnp.concatenate([by_head, tag], axis=0)
    ways, back = neighbours()
    arrived = [lax.ppermute(packed, THREAD, way) for way in ways]
    caches = (key_cache[0, :, 0], value_cache[0, :, 0], new_key[0, :, 0], new_value[0, :, 0])
    cache_space = [pltpu.VMEM(one.shape, one.dtype) for one in caches]
    cache_space.append(pltpu.SemaphoreType.DMA((len(caches),)))
    own, own_log = pl.pallas_call(
        own_kernel,
        out_shape=[jax.ShapeDtypeStruct((rows, head_dim), jnp.float32)] * 2,
        in_specs=[SCALAR] + on_chip(1) + [IN_HBM] * 4,
        out_specs=on_chip(2),
        scratch_shapes=cache_space,
        compiler_params=PARAMS,
        name="own",
    )(cache_len, by_head, *caches)
    weights = (out_weight, swap(out_weight, "zl", 1))
    parts = pl.pallas_call(
        near_kernel,
        out_shape=[jax.ShapeDtypeStruct(packed.shape, jnp.bfloat16)] * len(ways),
        in_specs=[SCALAR] + on_chip(1) + [IN_HBM] * 4 + on_chip(len(ways)),
        out_specs=on_chip(len(ways)),
        scratch_shapes=cache_space,
        compiler_params=PARAMS,
        name="near",
    )(cache_len, tag, *caches, *arrived)
    returned = [lax.ppermute(parts[back[way]], THREAD, ways[way]) for way in range(len(ways))]
    tags = [one[rows:] for one in arrived]
    attended, stack = pl.pallas_call(
        functools.partial(merge_kernel, len(ways)),
        out_shape=[
            jax.ShapeDtypeStruct((new_count, group_size * head_dim), jnp.bfloat16),
            jax.ShapeDtypeStruct(
                (lax.axis_size("x"), len(weights)) + out_weight.shape, out_weight.dtype
            ),
        ],
        in_specs=on_chip(3 + 2 * len(ways) + len(weights)),
        out_specs=on_chip(1) + [IN_HBM],
        scratch_shapes=[pltpu.SemaphoreType.DMA((lax.axis_size("x") * len(weights),))],
        compiler_params=PARAMS,
        name="merge",
    )(tag, own, own_log, *tags, *returned, *weights)
    return project(attended, stack)


def solution(mesh):
    fine = jax.sharding.Mesh(
        mesh.devices.reshape([size for _, size in FINE]), [name for name, _ in FINE]
    )
    placed = (
        P(THREAD),
        P(THREAD),
        P(THREAD, None, HEAD, None),
        P(THREAD, None, HEAD, None),
        P(THREAD, None, HEAD, None),
        P(THREAD, None, HEAD, None),
        P(THREAD, None, HEAD, None),
        P(HEAD, THREAD),
    )
    return jax.shard_map(
        body, mesh=fine, in_specs=placed, out_specs=P(None, HEAD, THREAD), check_vma=False
    )
```

```python
import functools

import jax
import jax.numpy as jnp
from jax import lax
from jax.experimental import pallas as pl
from jax.experimental.pallas import tpu as pltpu
from jax.sharding import PartitionSpec as P

STEP_TOK = 16
NEGATIVE = -1e30
LOG2_E = 1.4426950408889634
VMEM_LIMIT = 40 * 1024 * 1024

FINE = (("zt", 2), ("zm", 2), ("zl", 2), ("x", 4), ("c", 2), ("w", 2), ("y", 4))
THREAD = ("zt", "zm", "zl", "x", "c")
HEAD = ("w", "y")

BLOCK = 256
PAD = 16
LANES = 128


def diagonal(size):
    rows = lax.broadcasted_iota(jnp.int32, (size, size), 0)
    return rows == lax.broadcasted_iota(jnp.int32, (size, size), 1)


def attend_block(queries, first_row, keys, values, fresh_keys, fresh_values, length, is_own):
    factor = queries.shape[1] ** (-0.5)
    contract = (((1,), (1,)), ((), ()))
    cached = lax.dot_general(queries, keys, contract, preferred_element_type=jnp.float32)
    fresh = lax.dot_general(queries, fresh_keys, contract, preferred_element_type=jnp.float32)
    position = lax.broadcasted_iota(jnp.int32, (1, cached.shape[1]), 1)
    cached = cached + jnp.where(position < length, 0.0, NEGATIVE)
    new_count = fresh.shape[1]
    token = (first_row + lax.broadcasted_iota(jnp.int32, fresh.shape, 0)) % new_count
    key_token = lax.broadcasted_iota(jnp.int32, fresh.shape, 1)
    if is_own:
        allowed = key_token <= token
    else:
        allowed = key_token // STEP_TOK < token // STEP_TOK
    fresh = jnp.where(allowed, fresh, NEGATIVE)
    row_max = jnp.maximum(
        jnp.max(cached, axis=1, keepdims=True), jnp.max(fresh, axis=1, keepdims=True)
    )
    cached = jnp.exp2((cached - row_max) * (factor * LOG2_E))
    fresh = jnp.exp2((fresh - row_max) * (factor * LOG2_E))
    wide = jnp.concatenate([values, jnp.ones_like(values)], axis=1)
    summed = jnp.dot(cached.astype(jnp.bfloat16), wide, preferred_element_type=jnp.float32)
    wide = jnp.concatenate([fresh_values, jnp.ones_like(fresh_values)], axis=1)
    summed += jnp.dot(fresh.astype(jnp.bfloat16), wide, preferred_element_type=jnp.float32)
    total = summed[:, LANES:]
    return summed[:, :LANES] / total, row_max * factor + jnp.log(total)


def load(pairs, sems):
    copies = [pltpu.make_async_copy(src, dst, sems.at[i]) for i, (src, dst) in enumerate(pairs)]
    for copy in copies:
        copy.start()
    return copies


def own_kernel(
    length_ref, query_ref, key_hbm, value_hbm, new_key_hbm, new_value_hbm, out_ref, log_ref,
    key_ref, value_ref, new_key_ref, new_value_ref, sems,
):
    for copy in load(
        ((key_hbm, key_ref), (value_hbm, value_ref), (new_key_hbm, new_key_ref), (new_value_hbm, new_value_ref)), sems
    ):
        copy.wait()
    for start in range(0, out_ref.shape[0], BLOCK):
        block = pl.ds(start, BLOCK)
        result, log_total = attend_block(
            query_ref[block], start, key_ref[...], value_ref[...], new_key_ref[...],
            new_value_ref[...], length_ref[0], True,
        )
        out_ref[block] = result
        log_ref[block] = log_total


def same_request(own_ref, other_ref):
    return jnp.max(jnp.abs(own_ref[...].astype(jnp.float32) - other_ref[...].astype(jnp.float32))) == 0.0


def near_kernel(length_ref, own_tag_ref, key_hbm, value_hbm, new_key_hbm, new_value_hbm, *refs):
    *refs, key_ref, value_ref, new_key_ref, new_value_ref, sems = refs
    for copy in load(
        ((key_hbm, key_ref), (value_hbm, value_ref), (new_key_hbm, new_key_ref), (new_value_hbm, new_value_ref)), sems
    ):
        copy.wait()
    count = len(refs) // 2
    rows = refs[0].shape[0] - PAD
    for query_ref, out_ref in zip(refs[:count], refs[count:]):
        sibling = same_request(own_tag_ref, query_ref.at[pl.ds(rows, PAD)])

        @pl.when(sibling)
        def _():
            lines = []
            for start in range(0, rows, BLOCK):
                result, log_total = attend_block(
                    query_ref[pl.ds(start, BLOCK)], start, key_ref[...], value_ref[...],
                    new_key_ref[...], new_value_ref[...], length_ref[0], False,
                )
                out_ref[pl.ds(start, BLOCK)] = result.astype(out_ref.dtype)
                for piece in range(0, BLOCK, LANES):
                    column = log_total[piece : piece + LANES]
                    lines.append(
                        jnp.sum(jnp.where(diagonal(LANES), column, 0.0), axis=0, keepdims=True)
                    )
            exact = jnp.concatenate(lines, axis=0)
            high = exact.astype(jnp.bfloat16).astype(jnp.float32)
            middle = (exact - high).astype(jnp.bfloat16).astype(jnp.float32)
            low = exact - high - middle
            parts = jnp.concatenate([high, middle, low, jnp.zeros_like(low)], axis=0)
            out_ref[pl.ds(rows, PAD)] = parts.astype(out_ref.dtype)

        @pl.when(jnp.logical_not(sibling))
        def _():
            out_ref[...] = jnp.zeros_like(out_ref)


def merge_kernel(own_tag_ref, own_ref, own_log_ref, *refs):
    count = (len(refs) - 1) // 2
    tag_refs, part_refs, out_ref = refs[:count], refs[count:-1], refs[-1]
    rows = own_ref.shape[0]
    tokens = out_ref.shape[0]
    lines = rows // LANES
    siblings, logs = [], []
    for tag_ref, part_ref in zip(tag_refs, part_refs):
        siblings.append(same_request(own_tag_ref, tag_ref))
        pieces = part_ref[pl.ds(rows, PAD)].astype(jnp.float32)
        exact = pieces[:lines] + pieces[lines : 2 * lines] + pieces[2 * lines : 3 * lines]
        logs.append(jnp.where(siblings[-1], exact, NEGATIVE))
    for line in range(lines):
        block = pl.ds(line * LANES, LANES)
        columns = [own_log_ref[block]]
        terms = [own_ref[block]]
        for sibling, log_total, part_ref in zip(siblings, logs, part_refs):
            spread = jnp.broadcast_to(log_total[line : line + 1], (LANES, LANES))
            column = jnp.sum(jnp.where(diagonal(LANES), spread, 0.0), axis=1, keepdims=True)
            columns.append(jnp.broadcast_to(column, (LANES, LANES)))
            terms.append(jnp.where(sibling, part_ref[block].astype(jnp.float32), 0.0))
        largest = functools.reduce(jnp.maximum, columns)
        shares = [jnp.exp(column - largest) for column in columns]
        total = functools.reduce(jnp.add, shares)
        summed = functools.reduce(jnp.add, [share * term for share, term in zip(shares, terms)])
        merged = (summed / total).astype(out_ref.dtype)
        for piece in range(0, LANES, tokens):
            group = (line * LANES + piece) // tokens
            out_ref[:, pl.ds(group * LANES, LANES)] = merged[piece : piece + tokens]


def copies_kernel(first_hbm, second_hbm, out_hbm, first_ref, second_ref, sems):
    pair = (first_ref, second_ref)
    for copy in load(((first_hbm, first_ref), (second_hbm, second_ref)), sems):
        copy.wait()
    sent = load([(pair[i], out_hbm.at[copy, i]) for copy in range(out_hbm.shape[0]) for i in range(2)], sems)
    for copy in sent:
        copy.wait()


def pack_kernel(request_ref, query_ref, packed_ref, tag_ref):
    tokens, heads, _ = query_ref.shape
    for head in range(heads):
        packed_ref[pl.ds(head * tokens, tokens)] = query_ref[:, head]
    tag = jnp.full(tag_ref.shape, request_ref[0] + 1, jnp.int32).astype(jnp.float32).astype(tag_ref.dtype)
    packed_ref[pl.ds(heads * tokens, PAD)] = tag
    tag_ref[...] = tag


def relay_kernel(in_ref, out_ref):
    out_ref[...] = in_ref[...]


def project_kernel(place_ref, weight_ref, *refs):
    piece_refs, (out_ref, lines_ref) = refs[:-2], refs[-2:]
    pieces, (tokens, feats) = len(piece_refs), piece_refs[0].shape
    y_size, w_size = out_ref.shape[2:4]
    piece = tokens // (y_size * w_size)
    span = pieces * piece
    for index, piece_ref in enumerate(piece_refs):
        first = pl.multiple_of((place_ref[0] ^ index) * tokens, tokens)
        lines_ref[pl.ds(first, tokens)] = piece_ref[...]
    for x in range(weight_ref.shape[0]):
        weights = jnp.concatenate([weight_ref[x, 0], weight_ref[x, 1]], axis=1)
        terms = jnp.dot(lines_ref[...], weights, preferred_element_type=jnp.float32)
        terms = terms.reshape(pieces, w_size, y_size, piece, 2 * LANES)
        for y in range(y_size):
            for w in range(w_size):
                far = place_ref[2] ^ w
                part = terms[:, w, y].reshape(span, 2 * LANES).astype(out_ref.dtype)
                for side in range(2):
                    out_ref[place_ref[1] ^ side ^ far, x, y, far] = part[:, side * LANES : (side + 1) * LANES]


def on_chip(count):
    return [pl.BlockSpec(memory_space=pltpu.VMEM)] * count


IN_HBM = pl.BlockSpec(memory_space=pltpu.HBM)
SCALAR = pl.BlockSpec(memory_space=pltpu.SMEM)
DEAR = pl.CostEstimate(flops=40_000_000_000, bytes_accessed=0, transcendentals=0)
PARAMS = pltpu.CompilerParams(vmem_limit_bytes=VMEM_LIMIT)


def neighbours():
    count = 1
    for name in THREAD:
        count *= lax.axis_size(name)
    both = lambda pairs: [pair for i, j in pairs for pair in ((i, j), (j, i))]
    return (
        both((i, i + 2) for i in range(count) if i % 4 < 2),
        both((i, i + 2) for i in range(count - 2) if i % 4 >= 2),
        both((i, i + 1) for i in range(1, count - 1, 2)),
        both((i, i + 1) for i in range(0, count, 2)),
    )


def swap(value, axis, bit):
    names = (axis,) if isinstance(axis, str) else axis
    count = 1
    for name in names:
        count *= lax.axis_size(name)
    return lax.ppermute(value, axis, [(i, i ^ bit) for i in range(count)])


def project(attended, stack):
    tokens = attended.shape[0]
    size = {name: count for name, count in FINE}
    at = {name: lax.axis_index(name) for name in size}
    weights = lax.all_to_all(stack, "x", 0, 0)
    over_t, over_m = swap(attended, "zt", 1), swap(attended, "zm", 1)
    over_t = pl.pallas_call(
        relay_kernel,
        out_shape=jax.ShapeDtypeStruct(over_t.shape, over_t.dtype),
        in_specs=on_chip(1),
        out_specs=on_chip(1)[0],
        compiler_params=PARAMS,
        cost_estimate=DEAR,
        name="relay",
    )(over_t)
    near = (attended, over_m, over_t, swap(over_t, "zm", 1))
    pieces = [piece for one in near for piece in (one, swap(one, "c", 1))]
    place = jnp.stack([at["zt"] * 4 + at["zm"] * 2 + at["c"], at["zl"], at["w"]]).astype(jnp.int32)
    piece, columns = tokens // (size["y"] * size["w"]), weights.shape[-1]
    block = (size["zl"], size["x"], size["y"], size["w"], len(pieces) * piece, columns)
    terms = pl.pallas_call(
        project_kernel,
        out_shape=jax.ShapeDtypeStruct(block, jnp.bfloat16),
        in_specs=[SCALAR] + on_chip(1 + len(pieces)),
        out_specs=on_chip(1)[0],
        scratch_shapes=[pltpu.VMEM((len(pieces) * tokens, attended.shape[1]), jnp.bfloat16)],
        compiler_params=PARAMS,
        name="project",
    )(place, weights, *pieces)
    terms = lax.all_to_all(terms.reshape((-1,) + block[3:]), ("zl", "x", "y"), 0, 0).reshape(block)
    terms = jnp.sum(terms.astype(jnp.float32), axis=2)
    arrived = swap(terms[:, :, 1].astype(jnp.bfloat16), ("zl", "w"), 3)
    result = (terms[:, :, 0] + arrived.astype(jnp.float32)).astype(jnp.bfloat16)
    result = result.reshape(
        size["zl"], size["x"], size["zt"], size["zm"], size["c"], piece, columns
    )
    return result.transpose(2, 3, 0, 1, 4, 5, 6).reshape(-1, piece, columns)


def body(request_id, cache_len, query, new_key, new_value, key_cache, value_cache, out_weight):
    new_count, group_size, head_dim = query.shape[1:]
    rows = new_count * group_size
    packed, tag = pl.pallas_call(
        pack_kernel,
        out_shape=[
            jax.ShapeDtypeStruct((rows + PAD, head_dim), jnp.bfloat16),
            jax.ShapeDtypeStruct((PAD, head_dim), jnp.bfloat16),
        ],
        in_specs=[SCALAR] + on_chip(1),
        out_specs=on_chip(2),
        compiler_params=PARAMS,
        cost_estimate=DEAR,
        name="pack",
    )(request_id, query[0])
    ways = neighbours()
    arrived = [lax.ppermute(packed, THREAD, way) for way in ways]
    caches = (key_cache[0, :, 0], value_cache[0, :, 0], new_key[0, :, 0], new_value[0, :, 0])
    cache_space = [pltpu.VMEM(one.shape, one.dtype) for one in caches]
    cache_space.append(pltpu.SemaphoreType.DMA((len(caches),)))
    own, own_log = pl.pallas_call(
        own_kernel,
        out_shape=[jax.ShapeDtypeStruct((rows, head_dim), jnp.float32)] * 2,
        in_specs=[SCALAR] + on_chip(1) + [IN_HBM] * 4,
        out_specs=on_chip(2),
        scratch_shapes=cache_space,
        compiler_params=PARAMS,
        name="own",
    )(cache_len, packed, *caches)
    weights = (out_weight, swap(out_weight, "zl", 1))
    parts = pl.pallas_call(
        near_kernel,
        out_shape=[jax.ShapeDtypeStruct(packed.shape, jnp.bfloat16)] * len(ways),
        in_specs=[SCALAR] + on_chip(1) + [IN_HBM] * 4 + on_chip(len(ways)),
        out_specs=on_chip(len(ways)),
        scratch_shapes=cache_space,
        compiler_params=PARAMS,
        name="near",
    )(cache_len, tag, *caches, *arrived)
    returned = [lax.ppermute(part, THREAD, way) for part, way in zip(parts, ways)]
    tags = [one[rows:] for one in arrived]
    attended = pl.pallas_call(
        merge_kernel,
        out_shape=jax.ShapeDtypeStruct((new_count, group_size * head_dim), jnp.bfloat16),
        in_specs=on_chip(3 + 2 * len(ways)),
        out_specs=on_chip(1)[0],
        compiler_params=PARAMS,
        name="merge",
    )(tag, own, own_log, *tags, *returned)
    stack = pl.pallas_call(
        copies_kernel,
        out_shape=jax.ShapeDtypeStruct((lax.axis_size("x"), 2) + out_weight.shape, out_weight.dtype),
        in_specs=[IN_HBM] * 2,
        out_specs=IN_HBM,
        scratch_shapes=[pltpu.VMEM(out_weight.shape, out_weight.dtype)] * 2
        + [pltpu.SemaphoreType.DMA((2 * lax.axis_size("x"),))],
        compiler_params=pltpu.CompilerParams(vmem_limit_bytes=62 * 1024 * 1024),
        name="copies",
    )(*weights)
    return project(attended, stack)


def solution(mesh):
    fine = jax.sharding.Mesh(
        mesh.devices.reshape([size for _, size in FINE]), [name for name, _ in FINE]
    )
    placed = (
        P(THREAD),
        P(THREAD),
        P(THREAD, None, HEAD, None),
        P(THREAD, None, HEAD, None),
        P(THREAD, None, HEAD, None),
        P(THREAD, None, HEAD, None),
        P(THREAD, None, HEAD, None),
        P(HEAD, THREAD),
    )
    return jax.shard_map(
        body, mesh=fine, in_specs=placed, out_specs=P(None, HEAD, THREAD), check_vma=False
    )
```

```python
import functools

import jax
import jax.numpy as jnp
from jax import lax
from jax.experimental import pallas as pl
from jax.experimental.pallas import tpu as pltpu
from jax.sharding import PartitionSpec as P

STEP_TOK = 16
NEGATIVE = -1e30
LOG2_E = 1.4426950408889634
VMEM_LIMIT = 40 * 1024 * 1024

FINE = (("zt", 2), ("zm", 2), ("zl", 2), ("x", 4), ("c", 2), ("w", 2), ("y", 4))
THREAD = ("zt", "zm", "zl", "x", "c")
HEAD = ("w", "y")

BLOCK = 256
PAD = 16
LANES = 128


def diagonal(size):
    rows = lax.broadcasted_iota(jnp.int32, (size, size), 0)
    return rows == lax.broadcasted_iota(jnp.int32, (size, size), 1)


def attend_block(queries, first_row, keys, values, fresh_keys, fresh_values, length, is_own):
    factor = queries.shape[1] ** (-0.5)
    contract = (((1,), (1,)), ((), ()))
    cached = lax.dot_general(queries, keys, contract, preferred_element_type=jnp.float32)
    fresh = lax.dot_general(queries, fresh_keys, contract, preferred_element_type=jnp.float32)
    position = lax.broadcasted_iota(jnp.int32, (1, cached.shape[1]), 1)
    cached = cached + jnp.where(position < length, 0.0, NEGATIVE)
    new_count = fresh.shape[1]
    token = (first_row + lax.broadcasted_iota(jnp.int32, fresh.shape, 0)) % new_count
    key_token = lax.broadcasted_iota(jnp.int32, fresh.shape, 1)
    if is_own:
        allowed = key_token <= token
    else:
        allowed = key_token // STEP_TOK < token // STEP_TOK
    fresh = jnp.where(allowed, fresh, NEGATIVE)
    row_max = jnp.maximum(
        jnp.max(cached, axis=1, keepdims=True), jnp.max(fresh, axis=1, keepdims=True)
    )
    cached = jnp.exp2((cached - row_max) * (factor * LOG2_E))
    fresh = jnp.exp2((fresh - row_max) * (factor * LOG2_E))
    wide = jnp.concatenate([values, jnp.ones_like(values)], axis=1)
    summed = jnp.dot(cached.astype(jnp.bfloat16), wide, preferred_element_type=jnp.float32)
    wide = jnp.concatenate([fresh_values, jnp.ones_like(fresh_values)], axis=1)
    summed += jnp.dot(fresh.astype(jnp.bfloat16), wide, preferred_element_type=jnp.float32)
    total = summed[:, LANES:]
    return summed[:, :LANES] / total, row_max * factor + jnp.log(total)


def load(pairs, sems):
    copies = [pltpu.make_async_copy(src, dst, sems.at[i]) for i, (src, dst) in enumerate(pairs)]
    for copy in copies:
        copy.start()
    return copies


def own_kernel(
    length_ref, query_ref, key_hbm, value_hbm, new_key_hbm, new_value_hbm, weight_hbm, out_ref, log_ref,
    key_ref, value_ref, new_key_ref, new_value_ref, sems,
):
    for copy in load(
        ((key_hbm, key_ref), (value_hbm, value_ref), (new_key_hbm, new_key_ref), (new_value_hbm, new_value_ref)), sems
    ):
        copy.wait()
    del weight_hbm
    for filled, keys in cache_sizes(length_ref[0], key_ref.shape[0]):

        @pl.when(filled)
        def _():
            for start in range(0, out_ref.shape[0], BLOCK):
                block = pl.ds(start, BLOCK)
                result, log_total = attend_block(
                    query_ref[block], start, key_ref[keys], value_ref[keys], new_key_ref[...],
                    new_value_ref[...], length_ref[0], True,
                )
                out_ref[block] = result
                log_ref[block] = log_total


def cache_sizes(length, capacity):
    sizes = (capacity // 4, capacity // 2, capacity)
    for less, size in zip((0,) + sizes, sizes):
        yield jnp.logical_and(length > less, length <= size), pl.ds(0, size)


def same_request(own_ref, other_ref):
    return jnp.max(jnp.abs(own_ref[...].astype(jnp.float32) - other_ref[...].astype(jnp.float32))) == 0.0


def near_kernel(length_ref, own_tag_ref, key_hbm, value_hbm, new_key_hbm, new_value_hbm, *refs):
    *refs, key_ref, value_ref, new_key_ref, new_value_ref, sems = refs
    for copy in load(
        ((key_hbm, key_ref), (value_hbm, value_ref), (new_key_hbm, new_key_ref), (new_value_hbm, new_value_ref)), sems
    ):
        copy.wait()
    count = len(refs) // 2
    rows = refs[0].shape[0] - PAD
    for query_ref, out_ref in zip(refs[:count], refs[count:]):
        sibling = same_request(own_tag_ref, query_ref.at[pl.ds(rows, PAD)])
        for filled, keys in cache_sizes(length_ref[0], key_ref.shape[0]):

            @pl.when(jnp.logical_and(sibling, filled))
            def _():
                lines = []
                for start in range(0, rows, BLOCK):
                    result, log_total = attend_block(
                        query_ref[pl.ds(start, BLOCK)], start, key_ref[keys], value_ref[keys],
                        new_key_ref[...], new_value_ref[...], length_ref[0], False,
                    )
                    out_ref[pl.ds(start, BLOCK)] = result.astype(out_ref.dtype)
                    for piece in range(0, BLOCK, LANES):
                        column = log_total[piece : piece + LANES]
                        lines.append(
                            jnp.sum(jnp.where(diagonal(LANES), column, 0.0), axis=0, keepdims=True)
                        )
                exact = jnp.concatenate(lines, axis=0)
                high = exact.astype(jnp.bfloat16).astype(jnp.float32)
                middle = (exact - high).astype(jnp.bfloat16).astype(jnp.float32)
                low = exact - high - middle
                parts = jnp.concatenate([high, middle, low, jnp.zeros_like(low)], axis=0)
                out_ref[pl.ds(rows, PAD)] = parts.astype(out_ref.dtype)

        @pl.when(jnp.logical_not(sibling))
        def _():
            out_ref[...] = jnp.zeros_like(out_ref)


def merge_kernel(own_tag_ref, own_ref, own_log_ref, *refs):
    count = (len(refs) - 1) // 2
    tag_refs, part_refs, out_ref = refs[:count], refs[count:-1], refs[-1]
    rows = own_ref.shape[0]
    tokens = out_ref.shape[0]
    lines = rows // LANES
    siblings, logs = [], []
    for tag_ref, part_ref in zip(tag_refs, part_refs):
        siblings.append(same_request(own_tag_ref, tag_ref))
        pieces = part_ref[pl.ds(rows, PAD)].astype(jnp.float32)
        exact = pieces[:lines] + pieces[lines : 2 * lines] + pieces[2 * lines : 3 * lines]
        logs.append(jnp.where(siblings[-1], exact, NEGATIVE))
    for line in range(lines):
        block = pl.ds(line * LANES, LANES)
        columns = [own_log_ref[block]]
        terms = [own_ref[block]]
        for sibling, log_total, part_ref in zip(siblings, logs, part_refs):
            spread = jnp.broadcast_to(log_total[line : line + 1], (LANES, LANES))
            column = jnp.sum(jnp.where(diagonal(LANES), spread, 0.0), axis=1, keepdims=True)
            columns.append(jnp.broadcast_to(column, (LANES, LANES)))
            terms.append(jnp.where(sibling, part_ref[block].astype(jnp.float32), 0.0))
        largest = functools.reduce(jnp.maximum, columns)
        shares = [jnp.exp(column - largest) for column in columns]
        total = functools.reduce(jnp.add, shares)
        summed = functools.reduce(jnp.add, [share * term for share, term in zip(shares, terms)])
        merged = (summed / total).astype(out_ref.dtype)
        for piece in range(0, LANES, tokens):
            group = (line * LANES + piece) // tokens
            out_ref[:, pl.ds(group * LANES, LANES)] = merged[piece : piece + tokens]


def copies_kernel(first_ref, second_ref, out_hbm, sems):
    pair = (first_ref, second_ref)
    for copy in load([(pair[i], out_hbm.at[to, i]) for to in range(out_hbm.shape[0]) for i in range(2)], sems):
        copy.wait()


def pack_kernel(request_ref, query_ref, packed_ref, tag_ref):
    tokens, heads, _ = query_ref.shape
    for head in range(heads):
        packed_ref[pl.ds(head * tokens, tokens)] = query_ref[:, head]
    tag = jnp.full(tag_ref.shape, request_ref[0] + 1, jnp.int32).astype(jnp.float32).astype(tag_ref.dtype)
    packed_ref[pl.ds(heads * tokens, PAD)] = tag
    tag_ref[...] = tag


def relay_kernel(in_ref, out_ref):
    out_ref[...] = in_ref[...]


def project_kernel(place_ref, weight_ref, *refs):
    piece_refs, (out_ref, lines_ref) = refs[:-2], refs[-2:]
    pieces, (tokens, feats) = len(piece_refs), piece_refs[0].shape
    y_size, w_size = out_ref.shape[1], out_ref.shape[3]
    piece = tokens // (y_size * w_size)
    span = pieces * piece
    for index, piece_ref in enumerate(piece_refs):
        first = pl.multiple_of((place_ref[0] ^ index) * tokens, tokens)
        lines_ref[pl.ds(first, tokens)] = piece_ref[...]
    for x in range(weight_ref.shape[0]):
        weights = jnp.concatenate([weight_ref[x, 0], weight_ref[x, 1]], axis=1)
        terms = jnp.dot(lines_ref[...], weights, preferred_element_type=jnp.float32)
        terms = terms.reshape(pieces, w_size, y_size, piece, 2 * LANES)
        for y in range(y_size):
            for w in range(w_size):
                far = place_ref[2] ^ w
                part = terms[:, w, y].reshape(span, 2 * LANES).astype(out_ref.dtype)
                for side in range(2):
                    out_ref[place_ref[1] ^ side ^ far, y, x, far] = part[:, side * LANES : (side + 1) * LANES]


def on_chip(count):
    return [pl.BlockSpec(memory_space=pltpu.VMEM)] * count


ANYWHERE = pl.BlockSpec(memory_space=pl.ANY)
IN_HBM = pl.BlockSpec(memory_space=pltpu.HBM)
SCALAR = pl.BlockSpec(memory_space=pltpu.SMEM)
DEAR = pl.CostEstimate(flops=40_000_000_000, bytes_accessed=0, transcendentals=0)
PARAMS = pltpu.CompilerParams(vmem_limit_bytes=VMEM_LIMIT)


def neighbours():
    count = 1
    for name in THREAD:
        count *= lax.axis_size(name)
    both = lambda pairs: [pair for i, j in pairs for pair in ((i, j), (j, i))]
    return (
        both((i, i + 2) for i in range(count) if i % 4 < 2),
        both((i, i + 2) for i in range(count - 2) if i % 4 >= 2),
        both((i, i + 1) for i in range(1, count - 1, 2)),
        both((i, i + 1) for i in range(0, count, 2)),
    )


def swap(value, axis, bit):
    names = (axis,) if isinstance(axis, str) else axis
    count = 1
    for name in names:
        count *= lax.axis_size(name)
    return lax.ppermute(value, axis, [(i, i ^ bit) for i in range(count)])


def project(attended, stack):
    tokens = attended.shape[0]
    size = {name: count for name, count in FINE}
    at = {name: lax.axis_index(name) for name in size}
    weights = lax.all_to_all(stack, "x", 0, 0)
    over_t, over_m = swap(attended, "zt", 1), swap(attended, "zm", 1)
    over_t = pl.pallas_call(
        relay_kernel,
        out_shape=jax.ShapeDtypeStruct(over_t.shape, over_t.dtype),
        in_specs=on_chip(1),
        out_specs=on_chip(1)[0],
        compiler_params=PARAMS,
        cost_estimate=DEAR,
        name="relay",
    )(over_t)
    near = (attended, over_m, over_t, swap(over_t, "zm", 1))
    pieces = [piece for one in near for piece in (one, swap(one, "c", 1))]
    place = jnp.stack([at["zt"] * 4 + at["zm"] * 2 + at["c"], at["zl"], at["w"]]).astype(jnp.int32)
    piece, columns = tokens // (size["y"] * size["w"]), weights.shape[-1]
    block = (size["zl"], size["y"], size["x"], size["w"], len(pieces) * piece, columns)
    terms = pl.pallas_call(
        project_kernel,
        out_shape=jax.ShapeDtypeStruct(block, jnp.bfloat16),
        in_specs=[SCALAR] + on_chip(1 + len(pieces)),
        out_specs=on_chip(1)[0],
        scratch_shapes=[pltpu.VMEM((len(pieces) * tokens, attended.shape[1]), jnp.bfloat16)],
        compiler_params=PARAMS,
        name="project",
    )(place, weights, *pieces)
    terms = lax.all_to_all(terms.reshape((-1,) + block[3:]), ("zl", "y", "x"), 0, 0).reshape(block)
    terms = jnp.sum(terms.astype(jnp.float32), axis=1)
    arrived = swap(terms[:, :, 1].astype(jnp.bfloat16), ("zl", "w"), 3)
    result = (terms[:, :, 0] + arrived.astype(jnp.float32)).astype(jnp.bfloat16)
    result = result.reshape(
        size["zl"], size["x"], size["zt"], size["zm"], size["c"], piece, columns
    )
    return result.transpose(2, 3, 0, 1, 4, 5, 6).reshape(-1, piece, columns)


def body(request_id, cache_len, query, new_key, new_value, key_cache, value_cache, out_weight):
    new_count, group_size, head_dim = query.shape[1:]
    rows = new_count * group_size
    packed, tag = pl.pallas_call(
        pack_kernel,
        out_shape=[
            jax.ShapeDtypeStruct((rows + PAD, head_dim), jnp.bfloat16),
            jax.ShapeDtypeStruct((PAD, head_dim), jnp.bfloat16),
        ],
        in_specs=[SCALAR] + on_chip(1),
        out_specs=on_chip(2),
        compiler_params=PARAMS,
        cost_estimate=DEAR,
        name="pack",
    )(request_id, query[0])
    ways = neighbours()
    arrived = [lax.ppermute(packed, THREAD, way) for way in ways]
    caches = (key_cache[0, :, 0], value_cache[0, :, 0], new_key[0, :, 0], new_value[0, :, 0])
    cache_space = [pltpu.VMEM(one.shape, one.dtype) for one in caches]
    cache_space.append(pltpu.SemaphoreType.DMA((len(caches),)))
    weights = (out_weight, swap(out_weight, "zl", 1))
    own, own_log = pl.pallas_call(
        own_kernel,
        out_shape=[jax.ShapeDtypeStruct((rows, head_dim), jnp.float32)] * 2,
        in_specs=[SCALAR] + on_chip(1) + [IN_HBM] * 4 + [ANYWHERE],
        out_specs=on_chip(2),
        scratch_shapes=cache_space,
        compiler_params=PARAMS,
        name="own",
    )(cache_len, packed, *caches, weights[1])
    parts = pl.pallas_call(
        near_kernel,
        out_shape=[jax.ShapeDtypeStruct(packed.shape, jnp.bfloat16)] * len(ways),
        in_specs=[SCALAR] + on_chip(1) + [IN_HBM] * 4 + on_chip(len(ways)),
        out_specs=on_chip(len(ways)),
        scratch_shapes=cache_space,
        compiler_params=PARAMS,
        name="near",
    )(cache_len, tag, *caches, *arrived)
    returned = [lax.ppermute(part, THREAD, way) for part, way in zip(parts, ways)]
    tags = [one[rows:] for one in arrived]
    attended = pl.pallas_call(
        merge_kernel,
        out_shape=jax.ShapeDtypeStruct((new_count, group_size * head_dim), jnp.bfloat16),
        in_specs=on_chip(3 + 2 * len(ways)),
        out_specs=on_chip(1)[0],
        compiler_params=PARAMS,
        name="merge",
    )(tag, own, own_log, *tags, *returned)
    stack = pl.pallas_call(
        copies_kernel,
        out_shape=jax.ShapeDtypeStruct((lax.axis_size("x"), 2) + out_weight.shape, out_weight.dtype),
        in_specs=on_chip(2),
        out_specs=IN_HBM,
        scratch_shapes=[pltpu.SemaphoreType.DMA((2 * lax.axis_size("x"),))],
        compiler_params=pltpu.CompilerParams(vmem_limit_bytes=62 * 1024 * 1024),
        name="copies",
    )(*weights)
    return project(attended, stack)


def solution(mesh):
    fine = jax.sharding.Mesh(
        mesh.devices.reshape([size for _, size in FINE]), [name for name, _ in FINE]
    )
    placed = (
        P(THREAD),
        P(THREAD),
        P(THREAD, None, HEAD, None),
        P(THREAD, None, HEAD, None),
        P(THREAD, None, HEAD, None),
        P(THREAD, None, HEAD, None),
        P(THREAD, None, HEAD, None),
        P(HEAD, THREAD),
    )
    return jax.shard_map(
        body, mesh=fine, in_specs=placed, out_specs=P(None, HEAD, THREAD), check_vma=False
    )
```

```python
import functools

import jax
import jax.numpy as jnp
from jax import lax
from jax.experimental import pallas as pl
from jax.experimental.pallas import tpu as pltpu
from jax.sharding import PartitionSpec as P

STEP_TOK = 16
NEGATIVE = -1e30
LOG2_E = 1.4426950408889634
VMEM_LIMIT = 40 * 1024 * 1024

FINE = (("zt", 2), ("zm", 2), ("zl", 2), ("x", 4), ("c", 2), ("w", 2), ("y", 4))
THREAD = ("zt", "zm", "zl", "x", "c")
HEAD = ("w", "y")

BLOCK = 256
PAD = 16
LANES = 128


def diagonal(size):
    rows = lax.broadcasted_iota(jnp.int32, (size, size), 0)
    return rows == lax.broadcasted_iota(jnp.int32, (size, size), 1)


def attend_block(queries, first_row, keys, values, fresh_keys, fresh_values, length, is_own):
    factor = queries.shape[1] ** (-0.5)
    contract = (((1,), (1,)), ((), ()))
    cached = lax.dot_general(queries, keys, contract, preferred_element_type=jnp.float32)
    fresh = lax.dot_general(queries, fresh_keys, contract, preferred_element_type=jnp.float32)
    position = lax.broadcasted_iota(jnp.int32, (1, cached.shape[1]), 1)
    cached = cached + jnp.where(position < length, 0.0, NEGATIVE)
    new_count = fresh.shape[1]
    token = (first_row + lax.broadcasted_iota(jnp.int32, fresh.shape, 0)) % new_count
    key_token = lax.broadcasted_iota(jnp.int32, fresh.shape, 1)
    if is_own:
        allowed = key_token <= token
    else:
        allowed = key_token // STEP_TOK < token // STEP_TOK
    fresh = jnp.where(allowed, fresh, NEGATIVE)
    row_max = jnp.maximum(
        jnp.max(cached, axis=1, keepdims=True), jnp.max(fresh, axis=1, keepdims=True)
    )
    cached = jnp.exp2((cached - row_max) * (factor * LOG2_E))
    fresh = jnp.exp2((fresh - row_max) * (factor * LOG2_E))
    wide = jnp.concatenate([values, jnp.ones_like(values)], axis=1)
    summed = jnp.dot(cached.astype(jnp.bfloat16), wide, preferred_element_type=jnp.float32)
    wide = jnp.concatenate([fresh_values, jnp.ones_like(fresh_values)], axis=1)
    summed += jnp.dot(fresh.astype(jnp.bfloat16), wide, preferred_element_type=jnp.float32)
    total = summed[:, LANES:]
    return summed[:, :LANES] / total, row_max * factor + jnp.log(total)


def load(pairs, sems):
    copies = [pltpu.make_async_copy(src, dst, sems.at[i]) for i, (src, dst) in enumerate(pairs)]
    for copy in copies:
        copy.start()
    return copies


def own_kernel(
    length_ref, query_ref, key_ref, value_ref, new_key_ref, new_value_ref, weight_hbm, out_ref, log_ref,
):
    del weight_hbm
    for filled, keys in cache_sizes(length_ref[0], key_ref.shape[0]):

        @pl.when(filled)
        def _():
            for start in range(0, out_ref.shape[0], BLOCK):
                block = pl.ds(start, BLOCK)
                result, log_total = attend_block(
                    query_ref[block], start, key_ref[keys], value_ref[keys], new_key_ref[...],
                    new_value_ref[...], length_ref[0], True,
                )
                out_ref[block] = result
                log_ref[block] = log_total


def cache_sizes(length, capacity):
    sizes = (capacity // 4, capacity // 2, capacity)
    for less, size in zip((0,) + sizes, sizes):
        yield jnp.logical_and(length > less, length <= size), pl.ds(0, size)


def same_request(own_ref, other_ref):
    return jnp.max(jnp.abs(own_ref[...].astype(jnp.float32) - other_ref[...].astype(jnp.float32))) == 0.0


def near_kernel(length_ref, own_tag_ref, key_ref, value_ref, new_key_ref, new_value_ref, *refs):
    count = len(refs) // 2
    rows = refs[0].shape[0] - PAD
    for query_ref, out_ref in zip(refs[:count], refs[count:]):
        sibling = same_request(own_tag_ref, query_ref.at[pl.ds(rows, PAD)])
        for filled, keys in cache_sizes(length_ref[0], key_ref.shape[0]):

            @pl.when(jnp.logical_and(sibling, filled))
            def _():
                lines = []
                for start in range(0, rows, BLOCK):
                    result, log_total = attend_block(
                        query_ref[pl.ds(start, BLOCK)], start, key_ref[keys], value_ref[keys],
                        new_key_ref[...], new_value_ref[...], length_ref[0], False,
                    )
                    out_ref[pl.ds(start, BLOCK)] = result.astype(out_ref.dtype)
                    for piece in range(0, BLOCK, LANES):
                        column = log_total[piece : piece + LANES]
                        lines.append(
                            jnp.sum(jnp.where(diagonal(LANES), column, 0.0), axis=0, keepdims=True)
                        )
                exact = jnp.concatenate(lines, axis=0)
                high = exact.astype(jnp.bfloat16).astype(jnp.float32)
                middle = (exact - high).astype(jnp.bfloat16).astype(jnp.float32)
                low = exact - high - middle
                parts = jnp.concatenate([high, middle, low, jnp.zeros_like(low)], axis=0)
                out_ref[pl.ds(rows, PAD)] = parts.astype(out_ref.dtype)

        @pl.when(jnp.logical_not(sibling))
        def _():
            out_ref[...] = jnp.zeros_like(out_ref)


def merge_kernel(own_tag_ref, own_ref, own_log_ref, *refs):
    count = (len(refs) - 1) // 2
    tag_refs, part_refs, out_ref = refs[:count], refs[count:-1], refs[-1]
    rows = own_ref.shape[0]
    tokens = out_ref.shape[0]
    lines = rows // LANES
    siblings, logs = [], []
    for tag_ref, part_ref in zip(tag_refs, part_refs):
        siblings.append(same_request(own_tag_ref, tag_ref))
        pieces = part_ref[pl.ds(rows, PAD)].astype(jnp.float32)
        exact = pieces[:lines] + pieces[lines : 2 * lines] + pieces[2 * lines : 3 * lines]
        logs.append(jnp.where(siblings[-1], exact, NEGATIVE))
    for line in range(lines):
        block = pl.ds(line * LANES, LANES)
        columns = [own_log_ref[block]]
        terms = [own_ref[block]]
        for sibling, log_total, part_ref in zip(siblings, logs, part_refs):
            spread = jnp.broadcast_to(log_total[line : line + 1], (LANES, LANES))
            column = jnp.sum(jnp.where(diagonal(LANES), spread, 0.0), axis=1, keepdims=True)
            columns.append(jnp.broadcast_to(column, (LANES, LANES)))
            terms.append(jnp.where(sibling, part_ref[block].astype(jnp.float32), 0.0))
        largest = functools.reduce(jnp.maximum, columns)
        shares = [jnp.exp(column - largest) for column in columns]
        total = functools.reduce(jnp.add, shares)
        summed = functools.reduce(jnp.add, [share * term for share, term in zip(shares, terms)])
        merged = (summed / total).astype(out_ref.dtype)
        for piece in range(0, LANES, tokens):
            group = (line * LANES + piece) // tokens
            out_ref[:, pl.ds(group * LANES, LANES)] = merged[piece : piece + tokens]


def copies_kernel(first_ref, second_ref, out_hbm, sems):
    pair = (first_ref, second_ref)
    for copy in load([(pair[i], out_hbm.at[to, i]) for to in range(out_hbm.shape[0]) for i in range(2)], sems):
        copy.wait()


def pack_kernel(request_ref, query_ref, packed_ref, tag_ref):
    tokens, heads, _ = query_ref.shape
    for head in range(heads):
        packed_ref[pl.ds(head * tokens, tokens)] = query_ref[:, head]
    tag = jnp.full(tag_ref.shape, request_ref[0] + 1, jnp.int32).astype(jnp.float32).astype(tag_ref.dtype)
    packed_ref[pl.ds(heads * tokens, PAD)] = tag
    tag_ref[...] = tag


def relay_kernel(in_ref, out_ref):
    out_ref[...] = in_ref[...]


def project_kernel(place_ref, weight_ref, *refs):
    piece_refs, (out_ref, lines_ref) = refs[:-2], refs[-2:]
    pieces, (tokens, feats) = len(piece_refs), piece_refs[0].shape
    y_size, w_size = out_ref.shape[1], out_ref.shape[3]
    piece = tokens // (y_size * w_size)
    span = pieces * piece
    for index, piece_ref in enumerate(piece_refs):
        first = pl.multiple_of((place_ref[0] ^ index) * tokens, tokens)
        lines_ref[pl.ds(first, tokens)] = piece_ref[...]
    for x in range(weight_ref.shape[0]):
        weights = jnp.concatenate([weight_ref[x, 0], weight_ref[x, 1]], axis=1)
        terms = jnp.dot(lines_ref[...], weights, preferred_element_type=jnp.float32)
        terms = terms.reshape(pieces, w_size, y_size, piece, 2 * LANES)
        for y in range(y_size):
            for w in range(w_size):
                far = place_ref[2] ^ w
                part = terms[:, w, y].reshape(span, 2 * LANES).astype(out_ref.dtype)
                for side in range(2):
                    out_ref[place_ref[1] ^ side ^ far, y, x, far] = part[:, side * LANES : (side + 1) * LANES]


def on_chip(count):
    return [pl.BlockSpec(memory_space=pltpu.VMEM)] * count


ANYWHERE = pl.BlockSpec(memory_space=pl.ANY)
IN_HBM = pl.BlockSpec(memory_space=pltpu.HBM)
SCALAR = pl.BlockSpec(memory_space=pltpu.SMEM)
DEAR = pl.CostEstimate(flops=40_000_000_000, bytes_accessed=0, transcendentals=0)
PARAMS = pltpu.CompilerParams(vmem_limit_bytes=VMEM_LIMIT)


def neighbours():
    count = 1
    for name in THREAD:
        count *= lax.axis_size(name)
    both = lambda pairs: [pair for i, j in pairs for pair in ((i, j), (j, i))]
    return (
        both((i, i + 2) for i in range(count) if i % 4 < 2),
        both((i, i + 2) for i in range(count - 2) if i % 4 >= 2),
        both((i, i + 1) for i in range(1, count - 1, 2)),
        both((i, i + 1) for i in range(0, count, 2)),
    )


def swap(value, axis, bit):
    names = (axis,) if isinstance(axis, str) else axis
    count = 1
    for name in names:
        count *= lax.axis_size(name)
    return lax.ppermute(value, axis, [(i, i ^ bit) for i in range(count)])


def project(attended, stack):
    tokens = attended.shape[0]
    size = {name: count for name, count in FINE}
    at = {name: lax.axis_index(name) for name in size}
    weights = lax.all_to_all(stack, "x", 0, 0)
    over_t, over_m = swap(attended, "zt", 1), swap(attended, "zm", 1)
    over_t = pl.pallas_call(
        relay_kernel,
        out_shape=jax.ShapeDtypeStruct(over_t.shape, over_t.dtype),
        in_specs=on_chip(1),
        out_specs=on_chip(1)[0],
        compiler_params=PARAMS,
        cost_estimate=DEAR,
        name="relay",
    )(over_t)
    near = (attended, over_m, over_t, swap(over_t, "zm", 1))
    pieces = [piece for one in near for piece in (one, swap(one, "c", 1))]
    place = jnp.stack([at["zt"] * 4 + at["zm"] * 2 + at["c"], at["zl"], at["w"]]).astype(jnp.int32)
    piece, columns = tokens // (size["y"] * size["w"]), weights.shape[-1]
    block = (size["zl"], size["y"], size["x"], size["w"], len(pieces) * piece, columns)
    terms = pl.pallas_call(
        project_kernel,
        out_shape=jax.ShapeDtypeStruct(block, jnp.bfloat16),
        in_specs=[SCALAR] + on_chip(1 + len(pieces)),
        out_specs=on_chip(1)[0],
        scratch_shapes=[pltpu.VMEM((len(pieces) * tokens, attended.shape[1]), jnp.bfloat16)],
        compiler_params=PARAMS,
        name="project",
    )(place, weights, *pieces)
    terms = lax.all_to_all(terms.reshape((-1,) + block[3:]), ("zl", "y", "x"), 0, 0).reshape(block)
    terms = jnp.sum(terms.astype(jnp.float32), axis=1)
    arrived = swap(terms[:, :, 1].astype(jnp.bfloat16), ("zl", "w"), 3)
    result = (terms[:, :, 0] + arrived.astype(jnp.float32)).astype(jnp.bfloat16)
    result = result.reshape(
        size["zl"], size["x"], size["zt"], size["zm"], size["c"], piece, columns
    )
    return result.transpose(2, 3, 0, 1, 4, 5, 6).reshape(-1, piece, columns)


def body(request_id, cache_len, query, new_key, new_value, key_cache, value_cache, out_weight):
    new_count, group_size, head_dim = query.shape[1:]
    rows = new_count * group_size
    packed, tag = pl.pallas_call(
        pack_kernel,
        out_shape=[
            jax.ShapeDtypeStruct((rows + PAD, head_dim), jnp.bfloat16),
            jax.ShapeDtypeStruct((PAD, head_dim), jnp.bfloat16),
        ],
        in_specs=[SCALAR] + on_chip(1),
        out_specs=on_chip(2),
        compiler_params=PARAMS,
        cost_estimate=DEAR,
        name="pack",
    )(request_id, query[0])
    ways = neighbours()
    arrived = [lax.ppermute(packed, THREAD, way) for way in ways]
    caches = (key_cache[0, :, 0], value_cache[0, :, 0], new_key[0, :, 0], new_value[0, :, 0])
    weights = (out_weight, swap(out_weight, "zl", 1))
    own, own_log = pl.pallas_call(
        own_kernel,
        out_shape=[jax.ShapeDtypeStruct((rows, head_dim), jnp.float32)] * 2,
        in_specs=[SCALAR] + on_chip(5) + [ANYWHERE],
        out_specs=on_chip(2),
        compiler_params=PARAMS,
        name="own",
    )(cache_len, packed, *caches, weights[1])
    parts = pl.pallas_call(
        near_kernel,
        out_shape=[jax.ShapeDtypeStruct(packed.shape, jnp.bfloat16)] * len(ways),
        in_specs=[SCALAR] + on_chip(5 + len(ways)),
        out_specs=on_chip(len(ways)),
        compiler_params=PARAMS,
        name="near",
    )(cache_len, tag, *caches, *arrived)
    returned = [lax.ppermute(part, THREAD, way) for part, way in zip(parts, ways)]
    tags = [one[rows:] for one in arrived]
    attended = pl.pallas_call(
        merge_kernel,
        out_shape=jax.ShapeDtypeStruct((new_count, group_size * head_dim), jnp.bfloat16),
        in_specs=on_chip(3 + 2 * len(ways)),
        out_specs=on_chip(1)[0],
        compiler_params=PARAMS,
        name="merge",
    )(tag, own, own_log, *tags, *returned)
    stack = pl.pallas_call(
        copies_kernel,
        out_shape=jax.ShapeDtypeStruct((lax.axis_size("x"), 2) + out_weight.shape, out_weight.dtype),
        in_specs=on_chip(2),
        out_specs=IN_HBM,
        scratch_shapes=[pltpu.SemaphoreType.DMA((2 * lax.axis_size("x"),))],
        compiler_params=pltpu.CompilerParams(vmem_limit_bytes=62 * 1024 * 1024),
        name="copies",
    )(*weights)
    return project(attended, stack)


def solution(mesh):
    fine = jax.sharding.Mesh(
        mesh.devices.reshape([size for _, size in FINE]), [name for name, _ in FINE]
    )
    placed = (
        P(THREAD),
        P(THREAD),
        P(THREAD, None, HEAD, None),
        P(THREAD, None, HEAD, None),
        P(THREAD, None, HEAD, None),
        P(THREAD, None, HEAD, None),
        P(THREAD, None, HEAD, None),
        P(HEAD, THREAD),
    )
    return jax.shard_map(
        body, mesh=fine, in_specs=placed, out_specs=P(None, HEAD, THREAD), check_vma=False
    )
```
